1024 devices in a mesh: mem: 4 (over z_hi), lat: 256 (over z_lo, y, x, core).
Axes of the slice: x: 4, y: 8, z: 16 (z_hi: 4, z_lo: 4; z = z_hi * 4 + z_lo), core: 2. Of those that a mesh axis runs over, the one named last changes fastest.
Arguments:
- states: bfloat16 [64, 5, 1024, 4, 128], P('mem', None, 'lat'), may hold values from -6 to 6
- src_ids: int32 [4, 8], P('mem'), may hold values from 0 to 15, as said below
- coarse_w: float32 [512, 16, 32, 64], P('lat', None, None, 'mem'), may hold values from -1 to 1
- lon_cell: int32 [128], replicated, may hold values from 0 to 14, as said below
- lon_frac: float32 [128], replicated, may hold values from 0 to 1
- viscosity: float32 [4, 128], replicated, may hold values from 0.02 to 0.25
Outputs:
- forecast: float32 [64, 5, 1024, 4, 128], P('mem', None, 'lat')
The draws below stay inside these ranges and needn't reach their ends.
Inputs may be any that keep to these rules, and one draw needn't show every extreme that they name: `src_ids`: each group's row names 8 different members of that group by their index within it. `lon_cell`: never falls along longitude.
All inputs are finite; a program needn't handle non-finite values.
Results may differ from the reference program's by a relative error of at most 0.0003.
Values may be sent and summed in bfloat16 or wider, within the bound.
No kernel may reach another device: no remote copies, remote signals or barrier semaphores. Data moves between devices by JAX's collectives and lax.ppermute only.
A program may use at most 128 MiB of HBM per device.

```python
import math
import jax
import jax.numpy as jnp
from jax import lax

F = 5
LEV = 4
NLON = 128
CLON = 16
LAT_DEV = 4
M_DEV = 16
S_DEV = 8
GROUPS = 4
E = 64
S = 32
NLAT = 1024
CLAT = 512
N_LAT = 256


def draw_src_ids(key, part):
    key = jax.random.fold_in(key, 11)
    chosen = jax.random.randint(jax.random.fold_in(key, 1), (), 0, GROUPS)

    def one_group(group):
        sub = jax.random.fold_in(key, group + 7)
        drawn = jax.random.permutation(sub, M_DEV)[:S_DEV].astype(jnp.int32)
        inner = (1 + jax.random.permutation(jax.random.fold_in(sub, 3), M_DEV - 2)[:S_DEV - 2]).astype(jnp.int32)
        ends = jnp.array([0, M_DEV - 1], dtype=jnp.int32)
        forced = jnp.concatenate([ends, inner])
        forced = forced[jax.random.permutation(jax.random.fold_in(sub, 5), S_DEV)]
        return jnp.where(group == chosen, forced, drawn)
    return jax.vmap(one_group)(jnp.arange(GROUPS, dtype=jnp.int32))


def draw_lon_cell(key, part):
    key = jax.random.fold_in(key, 12)
    values = jax.random.randint(key, (NLON,), 0, CLON - 1)
    ordered = jnp.sort(values)
    ordered = ordered.at[0].set(0)
    ordered = ordered.at[NLON - 1].set(CLON - 2)
    return ordered.astype(jnp.int32)


def shard_levels(stream_key, extent, cuts, smallest, largest):
    factor_of, own = 1.0, jax.random.fold_in(stream_key, 6)
    for position, shards_of in cuts:
        heights = jnp.exp(jax.random.uniform(jax.random.fold_in(own, position), (shards_of,), jnp.float32, smallest / len(cuts), largest / len(cuts)))
        factor_of = factor_of * jnp.repeat(heights, extent[position] // shards_of).reshape([-1 if axis == position else 1 for axis in range(len(extent))])
    return factor_of


def normal_values(key, dims, scale, limit, pieces=(), kind=jnp.bfloat16):
    gain = shard_levels(key, dims, pieces, -0.22, 0.18) if pieces else 1.0
    entries = jax.random.normal(key, dims, jnp.float32) * scale * gain
    return jnp.minimum(jnp.maximum(entries, -limit), limit).astype(kind)


def setup_inputs(seed: int = 0) -> dict:
    seeds = jax.random.split(jax.random.key(seed), 7)
    states = normal_values(seeds[0], (E, F, NLAT, LEV, NLON), 1.0, 6.0, ((0, 4), (2, 256)))
    src_ids = draw_src_ids(jax.random.fold_in(seeds[6], 71), 0)
    coarse_w = normal_values(seeds[2], (CLAT, CLON, S, E), S ** -0.5, 1.0, ((0, 256), (3, 4)), jnp.float32)
    lon_cell = draw_lon_cell(jax.random.fold_in(seeds[6], 71), 0)
    lon_frac = jnp.clip(jax.random.uniform(seeds[4], (NLON,), jnp.float32, 0.0, 1.0), 0.0, 1.0)
    viscosity = jnp.clip(jnp.exp(jax.random.uniform(seeds[5], (LEV, NLON), jnp.float32, math.log(0.02), math.log(0.25))), 0.02, 0.25)
    return {"states": states, "src_ids": src_ids, "coarse_w": coarse_w, "lon_cell": lon_cell, "lon_frac": lon_frac, "viscosity": viscosity}


time_step = 0.25


def advance(padded, viscosity):
    centre = padded[..., 1:-1, :, :]
    north = padded[..., 2:, :, :]
    south = padded[..., :-2, :, :]
    east = jnp.roll(centre, -1, axis=-1)
    west = jnp.roll(centre, 1, axis=-1)
    dx_all = (east - west) * 0.5
    dy_all = (north - south) * 0.5
    lap_all = east + west + north + south - 4.0 * centre
    u_wind = centre[..., 0:1, :, :, :]
    v_wind = centre[..., 1:2, :, :, :]
    tend = -(u_wind * dx_all + v_wind * dy_all) + viscosity * lap_all
    zero_part = jnp.zeros_like(centre[..., 0:2, :, :, :])
    extra = jnp.concatenate([
        -dx_all[..., 2:3, :, :, :],
        -dy_all[..., 2:3, :, :, :],
        -(dx_all[..., 0:1, :, :, :] + dy_all[..., 1:2, :, :, :]),
        zero_part], axis=-4)
    return centre + time_step * (tend + extra)


def lon_matrix(lon_cell, lon_frac):
    points = jnp.arange(CLON, dtype=jnp.int32)
    lower = (lon_cell[:, None] == points[None, :])
    upper = ((lon_cell[:, None] + 1) == points[None, :])
    return jnp.where(lower, 1.0 - lon_frac[:, None], 0.0) + jnp.where(upper, lon_frac[:, None], 0.0)


def band_weights(coarse_band, table, rows):
    flat = coarse_band.reshape(2, CLON, -1)
    lon_w = jnp.einsum('nc,rcx->rnx', table, flat, precision=lax.Precision.HIGHEST)
    lon_w = lon_w.reshape(2, table.shape[0], coarse_band.shape[2], coarse_band.shape[3])
    frac = (jnp.arange(rows, dtype=jnp.float32) + 0.5) / rows
    return (1.0 - frac)[:, None, None, None] * lon_w[0][None] + frac[:, None, None, None] * lon_w[1][None]


def reference(states, src_ids, coarse_w, lon_cell, lon_frac, viscosity):
    flat = (jnp.arange(GROUPS, dtype=jnp.int32)[:, None] * M_DEV + src_ids).reshape(-1)
    sources = states[flat]
    sources = sources.reshape(S, F, N_LAT, LAT_DEV, LEV, NLON)
    sources = jnp.moveaxis(sources, 2, 0)
    coarse = coarse_w.reshape(N_LAT, 2, CLON, S, E)
    table = lon_matrix(lon_cell, lon_frac)

    def one_band(pair):
        src_band, coarse_band = pair
        weights = band_weights(coarse_band, table, LAT_DEV)
        return jnp.einsum('rnsk,sfrln->kfrln', weights, src_band.astype(jnp.float32), precision=lax.Precision.HIGHEST)

    analysis = lax.map(one_band, (sources, coarse))
    analysis = jnp.moveaxis(analysis, 0, 2).reshape(E, F, NLAT, LEV, NLON)

    def one_member(field):
        for step in range(2):
            padded = jnp.pad(field, ((0, 0), (1, 1), (0, 0), (0, 0)))
            field = advance(padded, viscosity)
        return field

    return lax.map(one_member, analysis)
```

```python
import functools

import jax
import jax.numpy as jnp
from jax import lax
from jax.experimental import pallas as pl
from jax.experimental.pallas import tpu as pltpu
from jax.sharding import PartitionSpec as P

ROWS = 4
LEV = 4
FIELDS = 5
VMEM_LIMIT = 48 * 1024 * 1024
VMEM = pl.BlockSpec(memory_space=pltpu.VMEM)
SMEM = pl.BlockSpec(memory_space=pltpu.SMEM)


def pick_kernel(ids_ref, states_ref, out_ref, sem):
    n = out_ref.shape[0]
    copies = []
    for i in range(n):
        copy = pltpu.make_async_copy(states_ref.at[ids_ref[0, i]], out_ref.at[i], sem.at[i])
        copy.start()
        copies.append(copy)
    for copy in copies:
        copy.wait()


def pick(states, src_ids):
    n = src_ids.shape[1]
    return pl.pallas_call(
        pick_kernel,
        out_shape=jax.ShapeDtypeStruct((n,) + states.shape[1:], states.dtype),
        in_specs=[SMEM, pl.BlockSpec(memory_space=pl.ANY)],
        out_specs=pl.BlockSpec(memory_space=pl.ANY),
        scratch_shapes=[pltpu.SemaphoreType.DMA((n,))],
        name="pick",
    )(src_ids, states)


def make_weights(coarse_ref, cell_ref, frac_ref, weights_ref, members):
    nlon = cell_ref.shape[1]
    points = coarse_ref.shape[0] // (2 * members)
    point = lax.broadcasted_iota(jnp.int32, (points, nlon), 0)
    cell = jnp.broadcast_to(cell_ref[...], (points, nlon))
    frac = jnp.broadcast_to(frac_ref[...], (points, nlon))
    table = jnp.where(cell == point, 1.0 - frac, 0.0) + jnp.where(cell + 1 == point, frac, 0.0)
    low, high = [], []
    for y in range(ROWS):
        t = (y + 0.5) / ROWS
        low.append((1.0 - t) * table)
        high.append(t * table)
    both = jnp.concatenate([jnp.concatenate(low, axis=1), jnp.concatenate(high, axis=1)], axis=0)
    for k in range(members):
        rows = coarse_ref[pl.ds(k, 2 * points, stride=members), :]
        product = lax.dot_general(
            rows, both, (((0,), (0,)), ((), ())),
            precision=lax.Precision.HIGHEST, preferred_element_type=jnp.float32)
        weights_ref[k] = product.reshape(weights_ref.shape[1:])


def analysis_kernel(members, block, coarse_ref, cell_ref, frac_ref, sources_ref, first_ref, last_ref, weights_ref, wide_ref):
    sources = sources_ref.shape[0] // FIELDS
    nlon = cell_ref.shape[1]
    half = ROWS * LEV // 2
    make_weights(coarse_ref, cell_ref, frac_ref, weights_ref, members)
    wide_ref[...] = sources_ref[...].astype(jnp.float32)
    upper = lax.broadcasted_iota(jnp.int32, (half, nlon), 0) < LEV
    for pair, out_ref in enumerate((first_ref, last_ref)):
        lanes = [slice(y * nlon, (y + 1) * nlon) for y in (2 * pair, 2 * pair + 1)]

        def some_members(b, carry, pair=pair, out_ref=out_ref, lanes=lanes):
            totals = [[None] * FIELDS for _ in range(block)]
            for s in range(sources):
                fields = [wide_ref[s * FIELDS + f, pair * half:(pair + 1) * half, :] for f in range(FIELDS)]
                for j in range(block):
                    row = weights_ref.at[b * block + j, s // 8]
                    w = jnp.where(
                        upper,
                        jnp.broadcast_to(row[s % 8:s % 8 + 1, lanes[0]], (half, nlon)),
                        jnp.broadcast_to(row[s % 8:s % 8 + 1, lanes[1]], (half, nlon)))
                    for f in range(FIELDS):
                        term = w * fields[f]
                        totals[j][f] = term if s == 0 else totals[j][f] + term
            for j in range(block):
                for f in range(FIELDS):
                    out_ref[(b * block + j) * FIELDS + f] = totals[j][f]
            return carry

        lax.fori_loop(0, members // block, some_members, 0)


def analyse(coarse, cell, frac, sources, members):
    nlon = cell.shape[1]
    count = sources.shape[0] // FIELDS
    pair = jax.ShapeDtypeStruct((members * FIELDS, ROWS * LEV // 2, nlon), jnp.float32)
    return pl.pallas_call(
        functools.partial(analysis_kernel, members, 4),
        out_shape=(pair, pair),
        in_specs=[VMEM] * 4,
        out_specs=(VMEM, VMEM),
        scratch_shapes=[
            pltpu.VMEM((members, count // 8, 8, ROWS * nlon), jnp.float32),
            pltpu.VMEM(sources.shape, jnp.float32),
        ],
        compiler_params=pltpu.CompilerParams(vmem_limit_bytes=VMEM_LIMIT),
        name="analysis",
    )(coarse, cell, frac, sources)


def forecast_kernel(edges_ref, viscosity_ref, first_ref, last_ref, before_ref, after_ref, out_ref):
    half, nlon = first_ref.shape[1:]
    members = first_ref.shape[0] // FIELDS
    upper = lax.broadcasted_iota(jnp.int32, (half, nlon), 0) < LEV
    spread = 0.25 * jnp.concatenate([viscosity_ref[...]] * 2, axis=0)
    stay = 1.0 - 4.0 * spread
    keep = jnp.where(upper, edges_ref[1], edges_ref[0]) != 0

    def swap(a):
        return pltpu.roll(a, LEV, 0)

    def advance(centre, north, south):
        west = [pltpu.roll(a, 1, 1) for a in centre]
        east = [pltpu.roll(a, nlon - 1, 1) for a in centre]
        dx = [e - w for e, w in zip(east, west)]
        dy = [n - s for n, s in zip(north, south)]
        u, v = centre[0] * -0.125, centre[1] * -0.125
        out = []
        for f in range(FIELDS):
            around = (east[f] + west[f]) + (north[f] + south[f])
            out.append(stay * centre[f] + spread * around + (u * dx[f] + v * dy[f]))
        out[0] = out[0] - 0.125 * dx[2]
        out[1] = out[1] - 0.125 * dy[2]
        out[2] = out[2] - 0.125 * (dx[0] + dy[1])
        return out

    def one_member(k, carry):
        base = k * FIELDS
        fields = range(FIELDS)
        first = [first_ref[base + f] for f in fields]
        last = [last_ref[base + f] for f in fields]
        before = [before_ref[base + f] for f in fields]
        after = [after_ref[base + f] for f in fields]
        edge = [jnp.where(upper, after[f], before[f]) for f in fields]
        sf, sl = [swap(a) for a in first], [swap(a) for a in last]
        sb, sa = [swap(a) for a in before], [swap(a) for a in after]

        def mix(a, b):
            return [jnp.where(upper, x, y) for x, y in zip(a, b)]

        first1 = advance(first, mix(sf, sl), mix(sb, sf))
        last1 = advance(last, mix(sl, sa), mix(sf, sl))
        edge1 = advance(edge, mix(sa, sf), mix(sl, sb))
        edge1 = [jnp.where(keep, a, 0.0) for a in edge1]
        sf, sl, se = [swap(a) for a in first1], [swap(a) for a in last1], [swap(a) for a in edge1]
        first2 = advance(first1, mix(sf, sl), mix(se, sf))
        last2 = advance(last1, mix(sl, se), mix(sf, sl))
        for f in fields:
            out_ref[base + f, :half, :] = first2[f]
            out_ref[base + f, half:, :] = last2[f]
        return carry

    lax.fori_loop(0, members, one_member, 0)


def forecast(edges, viscosity, first, last, before, after):
    count, half, nlon = first.shape
    return pl.pallas_call(
        forecast_kernel,
        out_shape=jax.ShapeDtypeStruct((count, 2 * half, nlon), jnp.float32),
        in_specs=[SMEM] + [VMEM] * 5,
        out_specs=VMEM,
        compiler_params=pltpu.CompilerParams(vmem_limit_bytes=VMEM_LIMIT),
        name="forecast",
    )(edges, viscosity, first, last, before, after)


def on_device(states, src_ids, coarse_w, lon_cell, lon_frac, viscosity):
    members, fields, rows, lev, nlon = states.shape
    picked = pick(states.reshape(members, fields, rows * lev, nlon), src_ids)
    sources = lax.all_gather(picked, "mem")
    sources = sources.reshape(-1, rows * lev, nlon)
    coarse = jnp.swapaxes(coarse_w, 2, 3)
    coarse = coarse.reshape(-1, coarse.shape[3])
    first, last = analyse(coarse, lon_cell[None], lon_frac[None], sources, members)
    size = lax.axis_size("lat")
    up = [(i, i + 1) for i in range(size - 1)]
    down = [(i + 1, i) for i in range(size - 1)]
    before = lax.ppermute(last, "lat", up)
    after = lax.ppermute(first, "lat", down)
    place = lax.axis_index("lat")
    edges = jnp.stack([place != 0, place != size - 1]).astype(jnp.int32)
    out = forecast(edges, viscosity, first, last, before, after)
    return out.reshape(members, fields, rows, lev, nlon)


def solution(mesh):
    in_specs = (
        P("mem", None, "lat", None, None),
        P("mem", None),
        P("lat", None, None, "mem"),
        P(),
        P(),
        P(),
    )
    out_specs = P("mem", None, "lat", None, None)
    return jax.shard_map(
        on_device, mesh=mesh, in_specs=in_specs, out_specs=out_specs, check_vma=False
    )
```

```python
import functools

import jax
import jax.numpy as jnp
from jax import lax
from jax.experimental import pallas as pl
from jax.experimental.pallas import tpu as pltpu
from jax.sharding import PartitionSpec as P

ROWS = 4
LEV = 4
FIELDS = 5
GROUP = 2
PARTS = 4
VMEM_LIMIT = 48 * 1024 * 1024
VMEM = pl.BlockSpec(memory_space=pltpu.VMEM)
SMEM = pl.BlockSpec(memory_space=pltpu.SMEM)


def pick_kernel(ids_ref, states_ref, out_ref):
    for i in range(out_ref.shape[0]):
        out_ref[i] = states_ref[ids_ref[0, i]]


def pick(states, src_ids):
    return pl.pallas_call(
        pick_kernel,
        out_shape=jax.ShapeDtypeStruct((src_ids.shape[1],) + states.shape[1:], states.dtype),
        in_specs=[SMEM, VMEM],
        out_specs=VMEM,
        name="pick",
    )(src_ids, states)


def make_weights(pair, coarse_ref, cell_ref, frac_ref, weights_ref):
    members = weights_ref.shape[0]
    nlon = cell_ref.shape[1]
    points = coarse_ref.shape[0] // (2 * members)
    point = lax.broadcasted_iota(jnp.int32, (points, nlon), 0)
    cell = jnp.broadcast_to(cell_ref[...], (points, nlon))
    frac = jnp.broadcast_to(frac_ref[...], (points, nlon))
    table = jnp.where(cell == point, 1.0 - frac, 0.0) + jnp.where(cell + 1 == point, frac, 0.0)
    low, high = [], []
    for i in range(2):
        t = ((2 * pair + i).astype(jnp.float32) + 0.5) / ROWS
        low.append((1.0 - t) * table)
        high.append(t * table)
    both = jnp.concatenate([jnp.concatenate(low, axis=1), jnp.concatenate(high, axis=1)], axis=0)
    for k in range(members):
        rows = coarse_ref[pl.ds(k, 2 * points, stride=members), :]
        product = lax.dot_general(
            rows, both, (((0,), (0,)), ((), ())),
            precision=lax.Precision.HIGHEST, preferred_element_type=jnp.float32)
        weights_ref[k] = product.reshape(weights_ref.shape[1:])


def analysis_kernel(facing, block, *refs):
    odd_ref, coarse_ref, cell_ref, frac_ref, sources_ref, *out_refs = refs[:-2]
    weights_ref, wide_ref = refs[-2:]
    pair = odd_ref[0] if facing else 1 - odd_ref[0]
    count = sources_ref.shape[0]
    sources = count // FIELDS
    members = weights_ref.shape[0]
    half, nlon = out_refs[0].shape[1:]
    make_weights(pair, coarse_ref, cell_ref, frac_ref, weights_ref)
    upper = lax.broadcasted_iota(jnp.int32, (half, nlon), 0) < LEV
    later = jnp.full((half, nlon), pair, jnp.int32) != 0
    for i in range(count):
        whole = sources_ref[i].astype(jnp.float32)
        wide_ref[i] = jnp.where(later, whole[half:], whole[:half])
    share = members // len(out_refs)

    def some_members(b, carry, start, out_ref):
        totals = [[None] * FIELDS for _ in range(block)]
        for s in range(sources):
            fields = [wide_ref[s * FIELDS + f] for f in range(FIELDS)]
            for j in range(block):
                row = weights_ref.at[start + b * block + j, s // 8]
                low, high = [
                    jnp.broadcast_to(row[s % 8:s % 8 + 1, i * nlon:(i + 1) * nlon], (half, nlon)) for i in range(2)
                ]
                w = jnp.where(upper, low, high)
                for f in range(FIELDS):
                    term = w * fields[f]
                    totals[j][f] = term if s == 0 else totals[j][f] + term
        for j in range(block):
            for f in range(FIELDS):
                out_ref[(b * block + j) * FIELDS + f] = totals[j][f]
        return carry

    for i, out_ref in enumerate(out_refs):
        lax.fori_loop(0, share // block, functools.partial(some_members, start=i * share, out_ref=out_ref), 0)


def analyse(facing, pieces, odd, coarse, cell, frac, sources, members):
    nlon = cell.shape[1]
    half = ROWS * LEV // 2
    count = sources.shape[0]
    return pl.pallas_call(
        functools.partial(analysis_kernel, facing, 4),
        out_shape=[jax.ShapeDtypeStruct((members * FIELDS // pieces, half, nlon), jnp.float32)] * pieces,
        in_specs=[SMEM] + [VMEM] * 4,
        out_specs=[VMEM] * pieces,
        scratch_shapes=[
            pltpu.VMEM((members, count // FIELDS // 8, 8, 2 * nlon), jnp.float32),
            pltpu.VMEM((count, half, nlon), jnp.float32),
        ],
        compiler_params=pltpu.CompilerParams(vmem_limit_bytes=VMEM_LIMIT),
        cost_estimate=pl.CostEstimate(flops=2 * 10**10, bytes_accessed=2 * 10**7, transcendentals=0),
        name="analysis_outer" if facing else "analysis_inner",
    )(odd, coarse, cell, frac, sources)


def forecast_kernel(
    group, place_ref, viscosity_ref, inside_low_ref, inside_high_ref, outside_ref, inner_low_ref, inner_high_ref, outer_ref,
    out_ref, result_ref, sem
):
    half, nlon = outer_ref.shape[1:]
    count = outer_ref.shape[0]
    members = count // FIELDS
    upper = lax.broadcasted_iota(jnp.int32, (half, nlon), 0) < LEV
    spread = 0.25 * jnp.concatenate([viscosity_ref[...]] * 2, axis=0)
    stay = 1.0 - 4.0 * spread
    keep = jnp.where(upper, place_ref[1], place_ref[0]) != 0
    odd = jnp.full((half, nlon), place_ref[2], jnp.int32) != 0

    def swap(a):
        return pltpu.roll(a, LEV, 0)

    def advance(centre, north, south):
        west = [pltpu.roll(a, 1, 1) for a in centre]
        east = [pltpu.roll(a, nlon - 1, 1) for a in centre]
        dx = [e - w for e, w in zip(east, west)]
        dy = [n - s for n, s in zip(north, south)]
        u, v = centre[0] * -0.125, centre[1] * -0.125
        out = []
        for f in range(FIELDS):
            around = (east[f] + west[f]) + (north[f] + south[f])
            out.append(stay * centre[f] + spread * around + (u * dx[f] + v * dy[f]))
        out[0] = out[0] - 0.125 * dx[2]
        out[1] = out[1] - 0.125 * dy[2]
        out[2] = out[2] - 0.125 * (dx[0] + dy[1])
        return out

    def mix(a, b):
        return [jnp.where(upper, x, y) for x, y in zip(a, b)]

    def one_member(k, high):
        base = k * FIELDS
        near = base - (count // 2 if high else 0)
        inner_ref, inside_ref = (inner_high_ref, inside_high_ref) if high else (inner_low_ref, inside_low_ref)
        fields = range(FIELDS)
        outer = [outer_ref[base + f] for f in fields]
        inner = [inner_ref[near + f] for f in fields]
        outside = [outside_ref[base + f] for f in fields]
        inside = [inside_ref[near + f] for f in fields]
        first = [jnp.where(odd, inner[f], outer[f]) for f in fields]
        last = [jnp.where(odd, outer[f], inner[f]) for f in fields]
        before = [jnp.where(odd, inside[f], outside[f]) for f in fields]
        after = [jnp.where(odd, outside[f], inside[f]) for f in fields]
        edge = mix(after, before)
        sf, sl = [swap(a) for a in first], [swap(a) for a in last]
        sb, sa = [swap(a) for a in before], [swap(a) for a in after]
        first1 = advance(first, mix(sf, sl), mix(sb, sf))
        last1 = advance(last, mix(sl, sa), mix(sf, sl))
        edge1 = advance(edge, mix(sa, sf), mix(sl, sb))
        edge1 = [jnp.where(keep, a, 0.0) for a in edge1]
        sf, sl, se = [swap(a) for a in first1], [swap(a) for a in last1], [swap(a) for a in edge1]
        first2 = advance(first1, mix(sf, sl), mix(se, sf))
        last2 = advance(last1, mix(sl, se), mix(sf, sl))
        for f in fields:
            result_ref[base + f, :half, :] = first2[f]
            result_ref[base + f, half:, :] = last2[f]

    parts = sem.shape[0]
    copies = []
    for part in range(parts):
        def some(i, carry, part=part):
            for j in range(group):
                one_member(part * (members // parts) + i * group + j, part >= parts // 2)
            return carry

        lax.fori_loop(0, members // parts // group, some, 0)
        rows = pl.ds(part * (count // parts), count // parts)
        copy = pltpu.make_async_copy(result_ref.at[rows], out_ref.at[rows], sem.at[part])
        copy.start()
        copies.append(copy)
    for copy in copies:
        copy.wait()


def forecast(place, viscosity, inside, outside, inner, outer, group=GROUP, parts=PARTS):
    count, half, nlon = outer.shape
    return pl.pallas_call(
        functools.partial(forecast_kernel, group),
        out_shape=jax.ShapeDtypeStruct((count, 2 * half, nlon), jnp.float32),
        in_specs=[SMEM] + [VMEM] * 7,
        out_specs=pl.BlockSpec(memory_space=pl.ANY),
        scratch_shapes=[pltpu.VMEM((count, 2 * half, nlon), jnp.float32), pltpu.SemaphoreType.DMA((parts,))],
        compiler_params=pltpu.CompilerParams(vmem_limit_bytes=VMEM_LIMIT),
        name="forecast",
    )(place, viscosity, *inside, outside, *inner, outer)


def on_device(states, src_ids, coarse_w, lon_cell, lon_frac, viscosity):
    members, fields, rows, lev, nlon = states.shape
    size = lax.axis_size("lat")
    lat = lax.axis_index("lat")
    place = jnp.stack([lat != 0, lat != size - 1, lat % 2 != 0]).astype(jnp.int32)
    odd = place[2:]
    coarse = jnp.swapaxes(coarse_w, 2, 3)
    coarse = coarse.reshape(-1, coarse.shape[3])
    cell, frac = lon_cell[None], lon_frac[None]
    picked = pick(states.reshape(members, fields, rows * lev, nlon), src_ids)
    sources = lax.all_gather(picked, "mem")
    sources = sources.reshape(-1, rows * lev, nlon)
    across = [(i, i + 1) for i in range(1, size - 1, 2)]
    across += [(j, i) for i, j in across]
    within = [(i, i + 1) for i in range(0, size, 2)]
    within += [(j, i) for i, j in within]
    outer, = analyse(True, 1, odd, coarse, cell, frac, sources, members)
    outside = lax.ppermute(outer, "lat", across)
    inner = analyse(False, 2, odd, coarse, cell, frac, sources, members)
    inside = [lax.ppermute(a, "lat", within) for a in inner]
    out = forecast(place, viscosity, inside, outside, inner, outer)
    return out.reshape(members, fields, rows, lev, nlon)


def solution(mesh):
    in_specs = (
        P("mem", None, "lat", None, None),
        P("mem", None),
        P("lat", None, None, "mem"),
        P(),
        P(),
        P(),
    )
    out_specs = P("mem", None, "lat", None, None)
    return jax.shard_map(
        on_device, mesh=mesh, in_specs=in_specs, out_specs=out_specs, check_vma=False
    )
```

```python
import functools

import jax
import jax.numpy as jnp
from jax import lax
from jax.experimental import pallas as pl
from jax.experimental.pallas import tpu as pltpu
from jax.sharding import PartitionSpec as P

ROWS = 4
LEV = 4
FIELDS = 5
GROUP = 2
PAD = 1
PARTS = 4
VMEM_LIMIT = 48 * 1024 * 1024
VMEM = pl.BlockSpec(memory_space=pltpu.VMEM)
SMEM = pl.BlockSpec(memory_space=pltpu.SMEM)


def pick_kernel(ids_ref, states_ref, out_ref):
    for i in range(out_ref.shape[0]):
        out_ref[i] = states_ref[ids_ref[0, i]]


def pick(states, src_ids):
    return pl.pallas_call(
        pick_kernel,
        out_shape=jax.ShapeDtypeStruct((src_ids.shape[1],) + states.shape[1:], states.dtype),
        in_specs=[SMEM, VMEM],
        out_specs=VMEM,
        name="pick",
    )(src_ids, states)


def make_weights(pair, coarse_ref, cell_ref, frac_ref, weights_ref):
    members = weights_ref.shape[0]
    nlon = cell_ref.shape[1]
    points = coarse_ref.shape[0] // (2 * members)
    point = lax.broadcasted_iota(jnp.int32, (points, nlon), 0)
    cell = jnp.broadcast_to(cell_ref[...], (points, nlon))
    frac = jnp.broadcast_to(frac_ref[...], (points, nlon))
    table = jnp.where(cell == point, 1.0 - frac, 0.0) + jnp.where(cell + 1 == point, frac, 0.0)
    low, high = [], []
    for i in range(2):
        t = ((2 * pair + i).astype(jnp.float32) + 0.5) / ROWS
        low.append((1.0 - t) * table)
        high.append(t * table)
    both = jnp.concatenate([jnp.concatenate(low, axis=1), jnp.concatenate(high, axis=1)], axis=0)
    for k in range(members):
        rows = coarse_ref[pl.ds(k, 2 * points, stride=members), :]
        product = lax.dot_general(
            rows, both, (((0,), (0,)), ((), ())),
            precision=lax.Precision.HIGHEST, preferred_element_type=jnp.float32)
        weights_ref[k] = product.reshape(weights_ref.shape[1:])


def analysis_kernel(facing, block, *refs):
    place_ref, coarse_ref, cell_ref, frac_ref, sources_ref, *out_refs = refs[:-2]
    weights_ref, wide_ref = refs[-2:]
    pair = place_ref[2] if facing else 1 - place_ref[2]
    count = sources_ref.shape[0]
    sources = count // FIELDS
    members = weights_ref.shape[0]
    half, nlon = out_refs[0].shape[1:]
    make_weights(pair, coarse_ref, cell_ref, frac_ref, weights_ref)
    upper = lax.broadcasted_iota(jnp.int32, (half, nlon), 0) < LEV
    later = jnp.full((half, nlon), pair, jnp.int32) != 0
    for i in range(count):
        whole = sources_ref[i].astype(jnp.float32)
        wide_ref[i] = jnp.where(later, whole[half:], whole[:half])
    share = members // len(out_refs)

    def some_members(b, carry, start, out_ref):
        totals = [[None] * FIELDS for _ in range(block)]
        for s in range(sources):
            fields = [wide_ref[s * FIELDS + f] for f in range(FIELDS)]
            for j in range(block):
                row = weights_ref.at[start + b * block + j, s // 8]
                low, high = [
                    jnp.broadcast_to(row[s % 8:s % 8 + 1, i * nlon:(i + 1) * nlon], (half, nlon)) for i in range(2)
                ]
                w = jnp.where(upper, low, high)
                for f in range(FIELDS):
                    term = w * fields[f]
                    totals[j][f] = term if s == 0 else totals[j][f] + term
        for j in range(block):
            for f in range(FIELDS):
                out_ref[(b * block + j) * FIELDS + f] = totals[j][f]
        return carry

    if facing:
        out_refs[0][members * FIELDS:] = jnp.zeros((PAD, half, nlon), jnp.float32)
    for i, out_ref in enumerate(out_refs):
        lax.fori_loop(0, share // block, functools.partial(some_members, start=i * share, out_ref=out_ref), 0)


def analyse(facing, pieces, place, coarse, cell, frac, sources, members):
    nlon = cell.shape[1]
    half = ROWS * LEV // 2
    count = sources.shape[0]
    return pl.pallas_call(
        functools.partial(analysis_kernel, facing, 4),
        out_shape=[jax.ShapeDtypeStruct((members * FIELDS // pieces + (PAD if facing else 0), half, nlon), jnp.float32)] * pieces,
        in_specs=[SMEM] + [VMEM] * 4,
        out_specs=[VMEM] * pieces,
        scratch_shapes=[
            pltpu.VMEM((members, count // FIELDS // 8, 8, 2 * nlon), jnp.float32),
            pltpu.VMEM((count, half, nlon), jnp.float32),
        ],
        compiler_params=pltpu.CompilerParams(vmem_limit_bytes=VMEM_LIMIT),
        cost_estimate=pl.CostEstimate(flops=2 * 10**10, bytes_accessed=2 * 10**7, transcendentals=0),
        name="analysis_outer" if facing else "analysis_inner",
    )(place, coarse, cell, frac, sources)


def forecast_kernel(
    group, place_ref, viscosity_ref, inside_ref, outside_ref, inner_ref, outer_ref, out_ref, result_ref, sem
):
    count, half, nlon = inner_ref.shape
    members = count // FIELDS
    upper = lax.broadcasted_iota(jnp.int32, (half, nlon), 0) < LEV
    spread = 0.25 * jnp.concatenate([viscosity_ref[...]] * 2, axis=0)
    stay = 1.0 - 4.0 * spread
    keep = jnp.where(upper, place_ref[1], place_ref[0]) != 0
    odd = jnp.full((half, nlon), place_ref[2], jnp.int32) != 0

    def swap(a):
        return pltpu.roll(a, LEV, 0)

    def advance(centre, north, south):
        west = [pltpu.roll(a, 1, 1) for a in centre]
        east = [pltpu.roll(a, nlon - 1, 1) for a in centre]
        dx = [e - w for e, w in zip(east, west)]
        dy = [n - s for n, s in zip(north, south)]
        u, v = centre[0] * -0.125, centre[1] * -0.125
        out = []
        for f in range(FIELDS):
            around = (east[f] + west[f]) + (north[f] + south[f])
            out.append(stay * centre[f] + spread * around + (u * dx[f] + v * dy[f]))
        out[0] = out[0] - 0.125 * dx[2]
        out[1] = out[1] - 0.125 * dy[2]
        out[2] = out[2] - 0.125 * (dx[0] + dy[1])
        return out

    def mix(a, b):
        return [jnp.where(upper, x, y) for x, y in zip(a, b)]

    def one_member(k):
        base = k * FIELDS
        fields = range(FIELDS)
        outer = [outer_ref[base + f] for f in fields]
        inner = [inner_ref[base + f] for f in fields]
        outside = [outside_ref[base + f] for f in fields]
        inside = [inside_ref[base + f] for f in fields]
        first = [jnp.where(odd, inner[f], outer[f]) for f in fields]
        last = [jnp.where(odd, outer[f], inner[f]) for f in fields]
        before = [jnp.where(odd, inside[f], outside[f]) for f in fields]
        after = [jnp.where(odd, outside[f], inside[f]) for f in fields]
        edge = mix(after, before)
        sf, sl = [swap(a) for a in first], [swap(a) for a in last]
        sb, sa = [swap(a) for a in before], [swap(a) for a in after]
        first1 = advance(first, mix(sf, sl), mix(sb, sf))
        last1 = advance(last, mix(sl, sa), mix(sf, sl))
        edge1 = advance(edge, mix(sa, sf), mix(sl, sb))
        edge1 = [jnp.where(keep, a, 0.0) for a in edge1]
        sf, sl, se = [swap(a) for a in first1], [swap(a) for a in last1], [swap(a) for a in edge1]
        first2 = advance(first1, mix(sf, sl), mix(se, sf))
        last2 = advance(last1, mix(sl, se), mix(sf, sl))
        for f in fields:
            result_ref[base + f, :half, :] = first2[f]
            result_ref[base + f, half:, :] = last2[f]

    parts = sem.shape[0]
    copies = []
    for part in range(parts):
        def some(i, carry, part=part):
            for j in range(group):
                one_member(part * (members // parts) + i * group + j)
            return carry

        lax.fori_loop(0, members // parts // group, some, 0)
        rows = pl.ds(part * (count // parts), count // parts)
        copy = pltpu.make_async_copy(result_ref.at[rows], out_ref.at[rows], sem.at[part])
        copy.start()
        copies.append(copy)
    for copy in copies:
        copy.wait()


def forecast(place, viscosity, inside, outside, inner, outer, group=GROUP, parts=PARTS):
    count, half, nlon = inner.shape
    return pl.pallas_call(
        functools.partial(forecast_kernel, group),
        out_shape=jax.ShapeDtypeStruct((count, 2 * half, nlon), jnp.float32),
        in_specs=[SMEM] + [VMEM] * 5,
        out_specs=pl.BlockSpec(memory_space=pl.ANY),
        scratch_shapes=[pltpu.VMEM((count, 2 * half, nlon), jnp.float32), pltpu.SemaphoreType.DMA((parts,))],
        compiler_params=pltpu.CompilerParams(vmem_limit_bytes=VMEM_LIMIT),
        name="forecast",
    )(place, viscosity, inside, outside, inner, outer)


def on_device(states, src_ids, coarse_w, lon_cell, lon_frac, viscosity):
    members, fields, rows, lev, nlon = states.shape
    size = lax.axis_size("lat")
    lat = lax.axis_index("lat")
    place = jnp.stack([lat != 0, lat != size - 1, lat % 2 != 0]).astype(jnp.int32)
    coarse = jnp.swapaxes(coarse_w, 2, 3)
    coarse = coarse.reshape(-1, coarse.shape[3])
    cell, frac = lon_cell[None], lon_frac[None]
    picked = pick(states.reshape(members, fields, rows * lev, nlon), src_ids)
    sources = lax.all_gather(picked, "mem")
    sources = sources.reshape(-1, rows * lev, nlon)
    across = [(i, i + 1) for i in range(1, size - 1, 2)]
    across += [(j, i) for i, j in across]
    within = [(i, i + 1) for i in range(0, size, 2)]
    within += [(j, i) for i, j in within]
    outer, = analyse(True, 1, place, coarse, cell, frac, sources, members)
    outside = lax.ppermute(outer, "lat", across)
    inner, = analyse(False, 1, place, coarse, cell, frac, sources, members)
    inside = lax.ppermute(inner, "lat", within)
    out = forecast(place, viscosity, inside, outside, inner, outer)
    return out.reshape(members, fields, rows, lev, nlon)


def solution(mesh):
    in_specs = (
        P("mem", None, "lat", None, None),
        P("mem", None),
        P("lat", None, None, "mem"),
        P(),
        P(),
        P(),
    )
    out_specs = P("mem", None, "lat", None, None)
    return jax.shard_map(
        on_device, mesh=mesh, in_specs=in_specs, out_specs=out_specs, check_vma=False
    )
```

```python
import functools

import jax
import jax.numpy as jnp
from jax import lax
from jax.experimental import pallas as pl
from jax.experimental.pallas import tpu as pltpu
from jax.sharding import PartitionSpec as P

ROWS = 4
LEV = 4
FIELDS = 5
GROUP = 2
PAD = 1
PARTS = 4
VMEM_LIMIT = 48 * 1024 * 1024
VMEM = pl.BlockSpec(memory_space=pltpu.VMEM)
SMEM = pl.BlockSpec(memory_space=pltpu.SMEM)


def pick_kernel(ids_ref, states_ref, cell_ref, frac_ref, out_ref, table_ref):
    odd = lax.axis_index("lat") % 2
    make_table(odd, cell_ref, frac_ref, table_ref.at[0])
    make_table(1 - odd, cell_ref, frac_ref, table_ref.at[1])
    for i in range(out_ref.shape[0]):
        out_ref[i] = states_ref[ids_ref[0, i]]


def pick(states, src_ids, cell, frac, points):
    return pl.pallas_call(
        pick_kernel,
        out_shape=(
            jax.ShapeDtypeStruct((src_ids.shape[1],) + states.shape[1:], states.dtype),
            jax.ShapeDtypeStruct((2, 6 * points, 2 * cell.shape[1]), jnp.float32),
        ),
        in_specs=[SMEM, VMEM, VMEM, VMEM],
        out_specs=(VMEM, VMEM),
        name="pick",
    )(src_ids, states, cell, frac)


def halves(a):
    big = a.astype(jnp.bfloat16).astype(jnp.float32)
    return big, (a - big).astype(jnp.bfloat16).astype(jnp.float32)


def make_table(pair, cell_ref, frac_ref, table_ref):
    points, nlon = table_ref.shape[0] // 6, cell_ref.shape[1]
    point = lax.broadcasted_iota(jnp.int32, (points, nlon), 0)
    cell = jnp.broadcast_to(cell_ref[...], (points, nlon))
    frac = jnp.broadcast_to(frac_ref[...], (points, nlon))
    table = jnp.where(cell == point, 1.0 - frac, 0.0) + jnp.where(cell + 1 == point, frac, 0.0)
    low, high = [], []
    for i in range(2):
        t = ((2 * pair + i).astype(jnp.float32) + 0.5) / ROWS
        low.append((1.0 - t) * table)
        high.append(t * table)
    both = jnp.concatenate([jnp.concatenate(low, axis=1), jnp.concatenate(high, axis=1)], axis=0)
    big, small = halves(both)
    table_ref[:2 * points] = big
    table_ref[2 * points:4 * points] = small
    table_ref[4 * points:] = big


def make_weights(coarse_ref, table_ref, weights_ref):
    members = weights_ref.shape[0]
    table = table_ref[...]
    for k in range(members):
        big, small = halves(coarse_ref[pl.ds(k, table.shape[0] // 3, stride=members), :])
        rows = jnp.concatenate([big, big, small], axis=0)
        product = lax.dot_general(rows, table, (((0,), (0,)), ((), ())), preferred_element_type=jnp.float32)
        weights_ref[k] = product.reshape(weights_ref.shape[1:])


def analysis_kernel(facing, block, *refs):
    coarse_ref, table_ref, sources_ref, *out_refs = refs[:-2]
    weights_ref, wide_ref = refs[-2:]
    odd = lax.axis_index("lat") % 2
    pair = odd if facing else 1 - odd
    count = sources_ref.shape[0]
    sources = count // FIELDS
    members = weights_ref.shape[0]
    half, nlon = out_refs[0].shape[1:]
    make_weights(coarse_ref, table_ref.at[0 if facing else 1], weights_ref)
    upper = lax.broadcasted_iota(jnp.int32, (half, nlon), 0) < LEV
    later = jnp.full((half, nlon), pair, jnp.int32) != 0
    for i in range(count):
        whole = sources_ref[i].astype(jnp.float32)
        wide_ref[i] = jnp.where(later, whole[half:], whole[:half])
    share = members // len(out_refs)

    def some_members(b, carry, start, out_ref):
        totals = [[None] * FIELDS for _ in range(block)]
        for s in range(sources):
            fields = [wide_ref[s * FIELDS + f] for f in range(FIELDS)]
            for j in range(block):
                row = weights_ref.at[start + b * block + j, s // 8]
                low, high = [
                    jnp.broadcast_to(row[s % 8:s % 8 + 1, i * nlon:(i + 1) * nlon], (half, nlon)) for i in range(2)
                ]
                w = jnp.where(upper, low, high)
                for f in range(FIELDS):
                    term = w * fields[f]
                    totals[j][f] = term if s == 0 else totals[j][f] + term
        for j in range(block):
            for f in range(FIELDS):
                out_ref[(b * block + j) * FIELDS + f] = totals[j][f]
        return carry

    if facing:
        out_refs[0][members * FIELDS:] = jnp.zeros((PAD, half, nlon), jnp.float32)
    for i, out_ref in enumerate(out_refs):
        lax.fori_loop(0, share // block, functools.partial(some_members, start=i * share, out_ref=out_ref), 0)


def analyse(facing, coarse, table, sources, members):
    nlon = sources.shape[2]
    half = ROWS * LEV // 2
    count = sources.shape[0]
    return pl.pallas_call(
        functools.partial(analysis_kernel, facing, 4),
        out_shape=jax.ShapeDtypeStruct((members * FIELDS + (PAD if facing else 0), half, nlon), jnp.float32),
        in_specs=[VMEM] * 3,
        out_specs=VMEM,
        scratch_shapes=[
            pltpu.VMEM((members, count // FIELDS // 8, 8, 2 * nlon), jnp.float32),
            pltpu.VMEM((count, half, nlon), jnp.float32),
        ],
        compiler_params=pltpu.CompilerParams(vmem_limit_bytes=VMEM_LIMIT),
        cost_estimate=pl.CostEstimate(flops=2 * 10**10, bytes_accessed=2 * 10**7, transcendentals=0),
        name="analysis_outer" if facing else "analysis_inner",
    )(coarse, table, sources)


def forecast_kernel(
    group, viscosity_ref, inside_ref, outside_ref, inner_ref, outer_ref, out_ref, result_ref, sem
):
    count, half, nlon = inner_ref.shape
    members = count // FIELDS
    upper = lax.broadcasted_iota(jnp.int32, (half, nlon), 0) < LEV
    spread = 0.25 * jnp.concatenate([viscosity_ref[...]] * 2, axis=0)
    stay = 1.0 - 4.0 * spread
    lat = lax.axis_index("lat")
    keep = jnp.where(upper, lax.axis_size("lat") - 1 - lat, lat) != 0
    odd = jnp.full((half, nlon), lat % 2, jnp.int32) != 0

    def swap(a):
        return pltpu.roll(a, LEV, 0)

    def advance(centre, north, south):
        west = [pltpu.roll(a, 1, 1) for a in centre]
        east = [pltpu.roll(a, nlon - 1, 1) for a in centre]
        dx = [e - w for e, w in zip(east, west)]
        dy = [n - s for n, s in zip(north, south)]
        u, v = centre[0] * -0.125, centre[1] * -0.125
        out = []
        for f in range(FIELDS):
            around = (east[f] + west[f]) + (north[f] + south[f])
            out.append(stay * centre[f] + spread * around + (u * dx[f] + v * dy[f]))
        out[0] = out[0] - 0.125 * dx[2]
        out[1] = out[1] - 0.125 * dy[2]
        out[2] = out[2] - 0.125 * (dx[0] + dy[1])
        return out

    def mix(a, b):
        return [jnp.where(upper, x, y) for x, y in zip(a, b)]

    def one_member(k):
        base = k * FIELDS
        fields = range(FIELDS)
        outer = [outer_ref[base + f] for f in fields]
        inner = [inner_ref[base + f] for f in fields]
        outside = [outside_ref[base + f] for f in fields]
        inside = [inside_ref[base + f] for f in fields]
        first = [jnp.where(odd, inner[f], outer[f]) for f in fields]
        last = [jnp.where(odd, outer[f], inner[f]) for f in fields]
        before = [jnp.where(odd, inside[f], outside[f]) for f in fields]
        after = [jnp.where(odd, outside[f], inside[f]) for f in fields]
        edge = mix(after, before)
        sf, sl = [swap(a) for a in first], [swap(a) for a in last]
        sb, sa = [swap(a) for a in before], [swap(a) for a in after]
        first1 = advance(first, mix(sf, sl), mix(sb, sf))
        last1 = advance(last, mix(sl, sa), mix(sf, sl))
        edge1 = advance(edge, mix(sa, sf), mix(sl, sb))
        edge1 = [jnp.where(keep, a, 0.0) for a in edge1]
        sf, sl, se = [swap(a) for a in first1], [swap(a) for a in last1], [swap(a) for a in edge1]
        first2 = advance(first1, mix(sf, sl), mix(se, sf))
        last2 = advance(last1, mix(sl, se), mix(sf, sl))
        for f in fields:
            result_ref[base + f, :half, :] = first2[f]
            result_ref[base + f, half:, :] = last2[f]

    parts = sem.shape[0]
    copies = []
    for part in range(parts):
        def some(i, carry, part=part):
            for j in range(group):
                one_member(part * (members // parts) + i * group + j)
            return carry

        lax.fori_loop(0, members // parts // group, some, 0)
        rows = pl.ds(part * (count // parts), count // parts)
        copy = pltpu.make_async_copy(result_ref.at[rows], out_ref.at[rows], sem.at[part])
        copy.start()
        copies.append(copy)
    for copy in copies:
        copy.wait()


def forecast(viscosity, inside, outside, inner, outer, group=GROUP, parts=PARTS):
    count, half, nlon = inner.shape
    return pl.pallas_call(
        functools.partial(forecast_kernel, group),
        out_shape=jax.ShapeDtypeStruct((count, 2 * half, nlon), jnp.float32),
        in_specs=[VMEM] * 5,
        out_specs=pl.BlockSpec(memory_space=pl.ANY),
        scratch_shapes=[pltpu.VMEM((count, 2 * half, nlon), jnp.float32), pltpu.SemaphoreType.DMA((parts,))],
        compiler_params=pltpu.CompilerParams(vmem_limit_bytes=VMEM_LIMIT),
        name="forecast",
    )(viscosity, inside, outside, inner, outer)


def on_device(states, src_ids, coarse_w, lon_cell, lon_frac, viscosity):
    members, fields, rows, lev, nlon = states.shape
    size = lax.axis_size("lat")
    coarse = jnp.swapaxes(coarse_w, 2, 3)
    coarse = coarse.reshape(-1, coarse.shape[3])
    picked, table = pick(
        states.reshape(members, fields, rows * lev, nlon), src_ids, lon_cell[None], lon_frac[None], coarse_w.shape[1])
    sources = lax.all_gather(picked, "mem")
    sources = sources.reshape(-1, rows * lev, nlon)
    across = [(i, i + 1) for i in range(1, size - 1, 2)]
    across += [(j, i) for i, j in across]
    within = [(i, i + 1) for i in range(0, size, 2)]
    within += [(j, i) for i, j in within]
    outer = analyse(True, coarse, table, sources, members)
    outside = lax.ppermute(outer, "lat", across)
    inner = analyse(False, coarse, table, sources, members)
    inside = lax.ppermute(inner, "lat", within)
    out = forecast(viscosity, inside, outside, inner, outer)
    return out.reshape(members, fields, rows, lev, nlon)


def solution(mesh):
    in_specs = (
        P("mem", None, "lat", None, None),
        P("mem", None),
        P("lat", None, None, "mem"),
        P(),
        P(),
        P(),
    )
    out_specs = P("mem", None, "lat", None, None)
    return jax.shard_map(
        on_device, mesh=mesh, in_specs=in_specs, out_specs=out_specs, check_vma=False
    )
```

```python
import functools

import jax
import jax.numpy as jnp
from jax import lax
from jax.experimental import pallas as pl
from jax.experimental.pallas import tpu as pltpu
from jax.sharding import PartitionSpec as P

ROWS = 4
LEV = 4
FIELDS = 5
GROUP = 2
PAD = 1
PARTS = 4
VMEM_LIMIT = 48 * 1024 * 1024
VMEM = pl.BlockSpec(memory_space=pltpu.VMEM)
SMEM = pl.BlockSpec(memory_space=pltpu.SMEM)


def pick_kernel(ids_ref, states_ref, cell_ref, frac_ref, out_ref, table_ref):
    odd = lax.axis_index("lat") % 2
    make_table(odd, cell_ref, frac_ref, table_ref.at[0])
    make_table(1 - odd, cell_ref, frac_ref, table_ref.at[1])
    for i in range(out_ref.shape[0]):
        out_ref[i] = states_ref[ids_ref[0, i]]


def pick(states, src_ids, cell, frac, points):
    return pl.pallas_call(
        pick_kernel,
        out_shape=(
            jax.ShapeDtypeStruct((src_ids.shape[1],) + states.shape[1:], states.dtype),
            jax.ShapeDtypeStruct((2, 6 * points, 2 * cell.shape[1]), jnp.float32),
        ),
        in_specs=[SMEM, VMEM, VMEM, VMEM],
        out_specs=(VMEM, VMEM),
        name="pick",
    )(src_ids, states, cell, frac)


def halves(a):
    big = a.astype(jnp.bfloat16).astype(jnp.float32)
    return big, (a - big).astype(jnp.bfloat16).astype(jnp.float32)


def make_table(pair, cell_ref, frac_ref, table_ref):
    points, nlon = table_ref.shape[0] // 6, cell_ref.shape[1]
    point = lax.broadcasted_iota(jnp.int32, (points, nlon), 0)
    cell = jnp.broadcast_to(cell_ref[...], (points, nlon))
    frac = jnp.broadcast_to(frac_ref[...], (points, nlon))
    table = jnp.where(cell == point, 1.0 - frac, 0.0) + jnp.where(cell + 1 == point, frac, 0.0)
    low, high = [], []
    for i in range(2):
        t = ((2 * pair + i).astype(jnp.float32) + 0.5) / ROWS
        low.append((1.0 - t) * table)
        high.append(t * table)
    both = jnp.concatenate([jnp.concatenate(low, axis=1), jnp.concatenate(high, axis=1)], axis=0)
    big, small = halves(both)
    table_ref[:2 * points] = big
    table_ref[2 * points:4 * points] = small
    table_ref[4 * points:] = big


def make_weights(coarse_ref, table_ref, weights_ref):
    members = weights_ref.shape[0]
    table = table_ref[...]
    for k in range(members):
        big, small = halves(coarse_ref[pl.ds(k, table.shape[0] // 3, stride=members), :])
        rows = jnp.concatenate([big, big, small], axis=0)
        product = lax.dot_general(rows, table, (((0,), (0,)), ((), ())), preferred_element_type=jnp.float32)
        weights_ref[k] = product.reshape(weights_ref.shape[1:])


def analysis_kernel(facing, block, *refs):
    coarse_ref, table_ref, sources_ref, *out_refs = refs[:-2]
    weights_ref, wide_ref = refs[-2:]
    odd = lax.axis_index("lat") % 2
    pair = odd if facing else 1 - odd
    count = sources_ref.shape[0]
    sources = count // FIELDS
    members = weights_ref.shape[0]
    half, nlon = out_refs[0].shape[1:]
    make_weights(coarse_ref, table_ref.at[0 if facing else 1], weights_ref)
    upper = lax.broadcasted_iota(jnp.int32, (half, nlon), 0) < LEV
    later = jnp.full((half, nlon), pair, jnp.int32) != 0
    for i in range(count):
        whole = sources_ref[i].astype(jnp.float32)
        wide_ref[i] = jnp.where(later, whole[half:], whole[:half])
    share = members // len(out_refs)

    def some_members(b, carry, start, out_ref):
        totals = [[None] * FIELDS for _ in range(block)]
        for s in range(sources):
            fields = [wide_ref[s * FIELDS + f] for f in range(FIELDS)]
            for j in range(block):
                row = weights_ref.at[start + b * block + j, s // 8]
                low, high = [
                    jnp.broadcast_to(row[s % 8:s % 8 + 1, i * nlon:(i + 1) * nlon], (half, nlon)) for i in range(2)
                ]
                w = jnp.where(upper, low, high)
                for f in range(FIELDS):
                    term = w * fields[f]
                    totals[j][f] = term if s == 0 else totals[j][f] + term
        for j in range(block):
            for f in range(FIELDS):
                out_ref[(b * block + j) * FIELDS + f] = totals[j][f]
        return carry

    if facing:
        out_refs[0][members * FIELDS:] = jnp.zeros((PAD, half, nlon), jnp.float32)
    for i, out_ref in enumerate(out_refs):
        lax.fori_loop(0, share // block, functools.partial(some_members, start=i * share, out_ref=out_ref), 0)


def analyse(facing, coarse, table, sources, members):
    nlon = sources.shape[2]
    half = ROWS * LEV // 2
    count = sources.shape[0]
    return pl.pallas_call(
        functools.partial(analysis_kernel, facing, 4),
        out_shape=jax.ShapeDtypeStruct((members * FIELDS + (PAD if facing else 0), half, nlon), jnp.float32),
        in_specs=[VMEM] * 3,
        out_specs=VMEM,
        scratch_shapes=[
            pltpu.VMEM((members, count // FIELDS // 8, 8, 2 * nlon), jnp.float32),
            pltpu.VMEM((count, half, nlon), jnp.float32),
        ],
        compiler_params=pltpu.CompilerParams(vmem_limit_bytes=VMEM_LIMIT),
        cost_estimate=pl.CostEstimate(flops=2 * 10**10, bytes_accessed=2 * 10**7, transcendentals=0),
        name="analysis_outer" if facing else "analysis_inner",
    )(coarse, table, sources)


def constants(viscosity_ref, half, nlon):
    upper = lax.broadcasted_iota(jnp.int32, (half, nlon), 0) < LEV
    spread = 0.25 * jnp.concatenate([viscosity_ref[...]] * 2, axis=0)
    odd = jnp.full((half, nlon), lax.axis_index("lat") % 2, jnp.int32) != 0
    return upper, spread, odd


def swap(a):
    return pltpu.roll(a, LEV, 0)


def choose(mask, a, b):
    return [jnp.where(mask, x, y) for x, y in zip(a, b)]


def advance(spread, centre, north, south):
    stay = 1.0 - 4.0 * spread
    west = [pltpu.roll(a, 1, 1) for a in centre]
    east = [pltpu.roll(a, a.shape[1] - 1, 1) for a in centre]
    dx = [e - w for e, w in zip(east, west)]
    dy = [n - s for n, s in zip(north, south)]
    u, v = centre[0] * -0.125, centre[1] * -0.125
    out = []
    for f in range(FIELDS):
        around = (east[f] + west[f]) + (north[f] + south[f])
        out.append(stay * centre[f] + spread * around + (u * dx[f] + v * dy[f]))
    out[0] = out[0] - 0.125 * dx[2]
    out[1] = out[1] - 0.125 * dy[2]
    out[2] = out[2] - 0.125 * (dx[0] + dy[1])
    return out


def begin_kernel(group, viscosity_ref, inside_ref, inner_ref, outer_ref, first_ref, last_ref, near_ref):
    count, half, nlon = inner_ref.shape
    upper, spread, odd = constants(viscosity_ref, half, nlon)
    fields = range(FIELDS)

    def one_member(k):
        base = k * FIELDS
        outer = [outer_ref[base + f] for f in fields]
        inner = [inner_ref[base + f] for f in fields]
        inside = [swap(inside_ref[base + f]) for f in fields]
        first, last = choose(odd, inner, outer), choose(odd, outer, inner)
        before = [jnp.where(odd, a, 0.0) for a in inside]
        after = [jnp.where(odd, 0.0, a) for a in inside]
        sf, sl = [swap(a) for a in first], [swap(a) for a in last]
        middle = choose(upper, sf, sl)
        first1 = advance(spread, first, middle, choose(upper, before, sf))
        last1 = advance(spread, last, choose(upper, sl, after), middle)
        near = choose(upper, sl, sf)
        for f in fields:
            first_ref[base + f] = first1[f]
            last_ref[base + f] = last1[f]
            near_ref[base + f] = near[f]

    def some(i, carry):
        for j in range(group):
            one_member(i * group + j)
        return carry

    lax.fori_loop(0, count // FIELDS // group, some, 0)


def begin(viscosity, inside, inner, outer):
    return pl.pallas_call(
        functools.partial(begin_kernel, GROUP),
        out_shape=[jax.ShapeDtypeStruct(inner.shape, jnp.float32)] * 3,
        in_specs=[VMEM] * 4,
        out_specs=[VMEM] * 3,
        compiler_params=pltpu.CompilerParams(vmem_limit_bytes=VMEM_LIMIT),
        cost_estimate=pl.CostEstimate(flops=1, bytes_accessed=1, transcendentals=0),
        name="begin",
    )(viscosity, inside, inner, outer)


def finish_kernel(
    group, viscosity_ref, outside_ref, inside_ref, outer_ref, first_ref, last_ref, near_ref, out_ref, result_ref, sem
):
    count, half, nlon = near_ref.shape
    members = count // FIELDS
    upper, spread, odd = constants(viscosity_ref, half, nlon)
    lat = lax.axis_index("lat")
    keep = jnp.where(upper, lax.axis_size("lat") - 1 - lat, lat) != 0
    here = upper != odd
    sign = jnp.where(odd, 0.125, -0.125)
    fields = range(FIELDS)

    def one_member(k):
        base = k * FIELDS
        outside = [outside_ref[base + f] for f in fields]
        inside = [inside_ref[base + f] for f in fields]
        first1 = [first_ref[base + f] for f in fields]
        last1 = [last_ref[base + f] for f in fields]
        near = [near_ref[base + f] for f in fields]
        edge = choose(here, inside, outside)
        beyond = [swap(a) for a in choose(here, outside, inside)]
        added = [jnp.where(here, swap(a), 0.0) for a in edge]
        weight = spread - sign * outer_ref[base + 1]
        more = [weight * a for a in added]
        more[1] = more[1] - sign * added[2]
        more[2] = more[2] - sign * added[1]
        first1 = [jnp.where(odd, a, a + m) for a, m in zip(first1, more)]
        last1 = [jnp.where(odd, a + m, a) for a, m in zip(last1, more)]
        edge1 = advance(spread, edge, choose(upper, beyond, near), choose(upper, near, beyond))
        edge1 = [jnp.where(keep, a, 0.0) for a in edge1]
        sf, sl, se = [swap(a) for a in first1], [swap(a) for a in last1], [swap(a) for a in edge1]
        middle = choose(upper, sf, sl)
        first2 = advance(spread, first1, middle, choose(upper, se, sf))
        last2 = advance(spread, last1, choose(upper, sl, se), middle)
        for f in fields:
            result_ref[base + f, :half, :] = first2[f]
            result_ref[base + f, half:, :] = last2[f]

    parts = sem.shape[0]
    copies = []
    for part in range(parts):
        def some(i, carry, part=part):
            for j in range(group):
                one_member(part * (members // parts) + i * group + j)
            return carry

        lax.fori_loop(0, members // parts // group, some, 0)
        rows = pl.ds(part * (count // parts), count // parts)
        copy = pltpu.make_async_copy(result_ref.at[rows], out_ref.at[rows], sem.at[part])
        copy.start()
        copies.append(copy)
    for copy in copies:
        copy.wait()


def finish(viscosity, outside, inside, outer, first, last, near):
    count, half, nlon = near.shape
    return pl.pallas_call(
        functools.partial(finish_kernel, GROUP),
        out_shape=jax.ShapeDtypeStruct((count, 2 * half, nlon), jnp.float32),
        in_specs=[VMEM] * 7,
        out_specs=pl.BlockSpec(memory_space=pl.ANY),
        scratch_shapes=[pltpu.VMEM((count, 2 * half, nlon), jnp.float32), pltpu.SemaphoreType.DMA((PARTS,))],
        compiler_params=pltpu.CompilerParams(vmem_limit_bytes=VMEM_LIMIT),
        name="finish",
    )(viscosity, outside, inside, outer, first, last, near)


def on_device(states, src_ids, coarse_w, lon_cell, lon_frac, viscosity):
    members, fields, rows, lev, nlon = states.shape
    size = lax.axis_size("lat")
    coarse = jnp.swapaxes(coarse_w, 2, 3)
    coarse = coarse.reshape(-1, coarse.shape[3])
    picked, table = pick(
        states.reshape(members, fields, rows * lev, nlon), src_ids, lon_cell[None], lon_frac[None], coarse_w.shape[1])
    sources = lax.all_gather(picked, "mem")
    sources = sources.reshape(-1, rows * lev, nlon)
    across = [(i, i + 1) for i in range(1, size - 1, 2)]
    across += [(j, i) for i, j in across]
    within = [(i, i + 1) for i in range(0, size, 2)]
    within += [(j, i) for i, j in within]
    outer = analyse(True, coarse, table, sources, members)
    outside = lax.ppermute(outer, "lat", across)
    inner = analyse(False, coarse, table, sources, members)
    inside = lax.ppermute(inner, "lat", within)
    first, last, near = begin(viscosity, inside, inner, outer)
    out = finish(viscosity, outside, inside, outer, first, last, near)
    return out.reshape(members, fields, rows, lev, nlon)


def solution(mesh):
    in_specs = (
        P("mem", None, "lat", None, None),
        P("mem", None),
        P("lat", None, None, "mem"),
        P(),
        P(),
        P(),
    )
    out_specs = P("mem", None, "lat", None, None)
    return jax.shard_map(
        on_device, mesh=mesh, in_specs=in_specs, out_specs=out_specs, check_vma=False
    )
```

```python
import functools

import jax
import jax.numpy as jnp
from jax import lax
from jax.experimental import pallas as pl
from jax.experimental.pallas import tpu as pltpu
from jax.sharding import PartitionSpec as P

ROWS = 4
LEV = 4
FIELDS = 5
GROUP = 2
PAD = 1
PARTS = 4
VMEM_LIMIT = 48 * 1024 * 1024
VMEM = pl.BlockSpec(memory_space=pltpu.VMEM)
SMEM = pl.BlockSpec(memory_space=pltpu.SMEM)


def pick_kernel(ids_ref, states_ref, cell_ref, frac_ref, out_ref, table_ref):
    odd = lax.axis_index("lat") % 2
    make_table(odd, cell_ref, frac_ref, table_ref.at[0])
    make_table(1 - odd, cell_ref, frac_ref, table_ref.at[1])
    for i in range(out_ref.shape[0]):
        out_ref[i] = states_ref[ids_ref[0, i]]


def pick(states, src_ids, cell, frac, points):
    return pl.pallas_call(
        pick_kernel,
        out_shape=(
            jax.ShapeDtypeStruct((src_ids.shape[1],) + states.shape[1:], states.dtype),
            jax.ShapeDtypeStruct((2, 6 * points, 2 * cell.shape[1]), jnp.float32),
        ),
        in_specs=[SMEM, VMEM, VMEM, VMEM],
        out_specs=(VMEM, VMEM),
        name="pick",
    )(src_ids, states, cell, frac)


def halves(a):
    big = a.astype(jnp.bfloat16).astype(jnp.float32)
    return big, (a - big).astype(jnp.bfloat16).astype(jnp.float32)


def make_table(pair, cell_ref, frac_ref, table_ref):
    points, nlon = table_ref.shape[0] // 6, cell_ref.shape[1]
    point = lax.broadcasted_iota(jnp.int32, (points, nlon), 0)
    cell = jnp.broadcast_to(cell_ref[...], (points, nlon))
    frac = jnp.broadcast_to(frac_ref[...], (points, nlon))
    table = jnp.where(cell == point, 1.0 - frac, 0.0) + jnp.where(cell + 1 == point, frac, 0.0)
    low, high = [], []
    for i in range(2):
        t = ((2 * pair + i).astype(jnp.float32) + 0.5) / ROWS
        low.append((1.0 - t) * table)
        high.append(t * table)
    both = jnp.concatenate([jnp.concatenate(low, axis=1), jnp.concatenate(high, axis=1)], axis=0)
    big, small = halves(both)
    table_ref[:2 * points] = big
    table_ref[2 * points:4 * points] = small
    table_ref[4 * points:] = big


def make_weights(coarse_ref, table_ref, weights_ref):
    members = weights_ref.shape[0]
    table = table_ref[...]
    for k in range(members):
        big, small = halves(coarse_ref[pl.ds(k, table.shape[0] // 3, stride=members), :])
        rows = jnp.concatenate([big, big, small], axis=0)
        product = lax.dot_general(rows, table, (((0,), (0,)), ((), ())), preferred_element_type=jnp.float32)
        weights_ref[k] = product.reshape(weights_ref.shape[1:])


def analysis_kernel(facing, block, *refs):
    coarse_ref, table_ref, sources_ref, out_ref, send_ref, weights_ref, wide_ref = refs
    odd = lax.axis_index("lat") % 2
    pair = odd if facing else 1 - odd
    count = sources_ref.shape[0]
    sources = count // FIELDS
    members = weights_ref.shape[0]
    half, nlon = out_ref.shape[1:]
    make_weights(coarse_ref, table_ref.at[0 if facing else 1], weights_ref)
    upper = lax.broadcasted_iota(jnp.int32, (half, nlon), 0) < LEV
    later = jnp.full((half, nlon), pair, jnp.int32) != 0
    for i in range(count):
        whole = sources_ref[i].astype(jnp.float32)
        wide_ref[i] = jnp.where(later, whole[half:], whole[:half])
    near = upper != later

    def some_members(b, carry):
        totals = [[None] * FIELDS for _ in range(block)]
        for s in range(sources):
            fields = [wide_ref[s * FIELDS + f] for f in range(FIELDS)]
            for j in range(block):
                row = weights_ref.at[b * block + j, s // 8]
                low, high = [
                    jnp.broadcast_to(row[s % 8:s % 8 + 1, i * nlon:(i + 1) * nlon], (half, nlon)) for i in range(2)
                ]
                w = jnp.where(upper, low, high)
                for f in range(FIELDS):
                    term = w * fields[f]
                    totals[j][f] = term if s == 0 else totals[j][f] + term
        items = [totals[j][f] for j in range(block) for f in range(FIELDS)]
        for i, item in enumerate(items):
            out_ref[b * len(items) + i] = item
        for i in range(0, len(items), 4):
            tile = (b * len(items) + i) // 4 * 3
            four = items[i:i + 4]
            rest = [a - a.astype(jnp.bfloat16).astype(jnp.float32) for a in four]
            rest = [jnp.where(near, rest[j], swap(rest[j + 1])) for j in (0, 2)]
            for j, two in enumerate((four[:2], four[2:], rest)):
                send_ref[tile + j] = jnp.concatenate(two, axis=0).astype(jnp.bfloat16)
        return carry

    if facing:
        send_ref[send_ref.shape[0] - PAD:] = jnp.zeros((PAD, 2 * half, nlon), jnp.bfloat16)
    lax.fori_loop(0, members // block, some_members, 0)


def receive(near, send_ref, out_ref):
    half = out_ref.shape[1]

    def four(g, carry):
        tiles = [send_ref[3 * g + j].astype(jnp.float32) for j in range(3)]
        for i in range(4):
            rest = tiles[2][i // 2 * half:(i // 2 + 1) * half]
            rest = jnp.where(near, swap(rest) if i % 2 else rest, 0.0)
            out_ref[4 * g + i] = tiles[i // 2][i % 2 * half:(i % 2 + 1) * half] + rest
        return carry

    lax.fori_loop(0, out_ref.shape[0] // 4, four, 0, unroll=5)


def analyse(facing, coarse, table, sources, members):
    nlon = sources.shape[2]
    half = ROWS * LEV // 2
    count = sources.shape[0]
    return pl.pallas_call(
        functools.partial(analysis_kernel, facing, 4),
        out_shape=(
            jax.ShapeDtypeStruct((members * FIELDS, half, nlon), jnp.float32),
            jax.ShapeDtypeStruct((members * FIELDS // 4 * 3 + (PAD if facing else 0), 2 * half, nlon), jnp.bfloat16),
        ),
        in_specs=[VMEM] * 3,
        out_specs=(VMEM, VMEM),
        scratch_shapes=[
            pltpu.VMEM((members, count // FIELDS // 8, 8, 2 * nlon), jnp.float32),
            pltpu.VMEM((count, half, nlon), jnp.float32),
        ],
        compiler_params=pltpu.CompilerParams(vmem_limit_bytes=VMEM_LIMIT),
        cost_estimate=pl.CostEstimate(flops=2 * 10**10, bytes_accessed=2 * 10**7, transcendentals=0),
        name="analysis_outer" if facing else "analysis_inner",
    )(coarse, table, sources)


def constants(viscosity_ref, half, nlon):
    upper = lax.broadcasted_iota(jnp.int32, (half, nlon), 0) < LEV
    spread = 0.25 * jnp.concatenate([viscosity_ref[...]] * 2, axis=0)
    odd = jnp.full((half, nlon), lax.axis_index("lat") % 2, jnp.int32) != 0
    return upper, spread, odd


def swap(a):
    return pltpu.roll(a, LEV, 0)


def choose(mask, a, b):
    return [jnp.where(mask, x, y) for x, y in zip(a, b)]


def advance(spread, centre, north, south):
    stay = 1.0 - 4.0 * spread
    west = [pltpu.roll(a, 1, 1) for a in centre]
    east = [pltpu.roll(a, a.shape[1] - 1, 1) for a in centre]
    dx = [e - w for e, w in zip(east, west)]
    dy = [n - s for n, s in zip(north, south)]
    u, v = centre[0] * -0.125, centre[1] * -0.125
    out = []
    for f in range(FIELDS):
        around = (east[f] + west[f]) + (north[f] + south[f])
        out.append(stay * centre[f] + spread * around + (u * dx[f] + v * dy[f]))
    out[0] = out[0] - 0.125 * dx[2]
    out[1] = out[1] - 0.125 * dy[2]
    out[2] = out[2] - 0.125 * (dx[0] + dy[1])
    return out


def begin_kernel(group, viscosity_ref, sent_ref, inner_ref, outer_ref, first_ref, last_ref, near_ref, inside_ref):
    count, half, nlon = inner_ref.shape
    upper, spread, odd = constants(viscosity_ref, half, nlon)
    receive(upper != odd, sent_ref, inside_ref)
    fields = range(FIELDS)

    def one_member(k):
        base = k * FIELDS
        outer = [outer_ref[base + f] for f in fields]
        inner = [inner_ref[base + f] for f in fields]
        inside = [swap(inside_ref[base + f]) for f in fields]
        first, last = choose(odd, inner, outer), choose(odd, outer, inner)
        before = [jnp.where(odd, a, 0.0) for a in inside]
        after = [jnp.where(odd, 0.0, a) for a in inside]
        sf, sl = [swap(a) for a in first], [swap(a) for a in last]
        middle = choose(upper, sf, sl)
        first1 = advance(spread, first, middle, choose(upper, before, sf))
        last1 = advance(spread, last, choose(upper, sl, after), middle)
        near = choose(upper, sl, sf)
        for f in fields:
            first_ref[base + f] = first1[f]
            last_ref[base + f] = last1[f]
            near_ref[base + f] = near[f]

    def some(i, carry):
        for j in range(group):
            one_member(i * group + j)
        return carry

    lax.fori_loop(0, count // FIELDS // group, some, 0)


def begin(viscosity, inside, inner, outer):
    return pl.pallas_call(
        functools.partial(begin_kernel, GROUP),
        out_shape=[jax.ShapeDtypeStruct(inner.shape, jnp.float32)] * 4,
        in_specs=[VMEM] * 4,
        out_specs=[VMEM] * 4,
        compiler_params=pltpu.CompilerParams(vmem_limit_bytes=VMEM_LIMIT),
        cost_estimate=pl.CostEstimate(flops=1, bytes_accessed=1, transcendentals=0),
        name="begin",
    )(viscosity, inside, inner, outer)


def finish_kernel(
    group, viscosity_ref, sent_ref, inside_ref, outer_ref, first_ref, last_ref, near_ref,
    out_ref, outside_ref, result_ref, sem
):
    count, half, nlon = near_ref.shape
    members = count // FIELDS
    upper, spread, odd = constants(viscosity_ref, half, nlon)
    lat = lax.axis_index("lat")
    keep = jnp.where(upper, lax.axis_size("lat") - 1 - lat, lat) != 0
    here = upper != odd
    receive(upper == odd, sent_ref, outside_ref)
    sign = jnp.where(odd, 0.125, -0.125)
    fields = range(FIELDS)

    def one_member(k):
        base = k * FIELDS
        outside = [outside_ref[base + f] for f in fields]
        inside = [inside_ref[base + f] for f in fields]
        first1 = [first_ref[base + f] for f in fields]
        last1 = [last_ref[base + f] for f in fields]
        near = [near_ref[base + f] for f in fields]
        edge = choose(here, inside, outside)
        beyond = [swap(a) for a in choose(here, outside, inside)]
        added = [jnp.where(here, swap(a), 0.0) for a in edge]
        weight = spread - sign * outer_ref[base + 1]
        more = [weight * a for a in added]
        more[1] = more[1] - sign * added[2]
        more[2] = more[2] - sign * added[1]
        first1 = [jnp.where(odd, a, a + m) for a, m in zip(first1, more)]
        last1 = [jnp.where(odd, a + m, a) for a, m in zip(last1, more)]
        edge1 = advance(spread, edge, choose(upper, beyond, near), choose(upper, near, beyond))
        edge1 = [jnp.where(keep, a, 0.0) for a in edge1]
        sf, sl, se = [swap(a) for a in first1], [swap(a) for a in last1], [swap(a) for a in edge1]
        middle = choose(upper, sf, sl)
        first2 = advance(spread, first1, middle, choose(upper, se, sf))
        last2 = advance(spread, last1, choose(upper, sl, se), middle)
        for f in fields:
            result_ref[base + f, :half, :] = first2[f]
            result_ref[base + f, half:, :] = last2[f]

    parts = sem.shape[0]
    copies = []
    for part in range(parts):
        def some(i, carry, part=part):
            for j in range(group):
                one_member(part * (members // parts) + i * group + j)
            return carry

        lax.fori_loop(0, members // parts // group, some, 0)
        rows = pl.ds(part * (count // parts), count // parts)
        copy = pltpu.make_async_copy(result_ref.at[rows], out_ref.at[rows], sem.at[part])
        copy.start()
        copies.append(copy)
    for copy in copies:
        copy.wait()


def finish(viscosity, outside, inside, outer, first, last, near):
    count, half, nlon = near.shape
    return pl.pallas_call(
        functools.partial(finish_kernel, GROUP),
        out_shape=jax.ShapeDtypeStruct((count, 2 * half, nlon), jnp.float32),
        in_specs=[VMEM] * 7,
        out_specs=pl.BlockSpec(memory_space=pl.ANY),
        scratch_shapes=[
            pltpu.VMEM((count, half, nlon), jnp.float32),
            pltpu.VMEM((count, 2 * half, nlon), jnp.float32),
            pltpu.SemaphoreType.DMA((PARTS,)),
        ],
        compiler_params=pltpu.CompilerParams(vmem_limit_bytes=VMEM_LIMIT),
        name="finish",
    )(viscosity, outside, inside, outer, first, last, near)


def on_device(states, src_ids, coarse_w, lon_cell, lon_frac, viscosity):
    members, fields, rows, lev, nlon = states.shape
    size = lax.axis_size("lat")
    coarse = jnp.swapaxes(coarse_w, 2, 3)
    coarse = coarse.reshape(-1, coarse.shape[3])
    picked, table = pick(
        states.reshape(members, fields, rows * lev, nlon), src_ids, lon_cell[None], lon_frac[None], coarse_w.shape[1])
    sources = lax.all_gather(picked, "mem")
    sources = sources.reshape(-1, rows * lev, nlon)
    across = [(i, i + 1) for i in range(1, size - 1, 2)]
    across += [(j, i) for i, j in across]
    within = [(i, i + 1) for i in range(0, size, 2)]
    within += [(j, i) for i, j in within]
    outer, send = analyse(True, coarse, table, sources, members)
    outside = lax.ppermute(send, "lat", across)
    inner, send = analyse(False, coarse, table, sources, members)
    inside = lax.ppermute(send, "lat", within)
    first, last, near, inside = begin(viscosity, inside, inner, outer)
    out = finish(viscosity, outside, inside, outer, first, last, near)
    return out.reshape(members, fields, rows, lev, nlon)


def solution(mesh):
    in_specs = (
        P("mem", None, "lat", None, None),
        P("mem", None),
        P("lat", None, None, "mem"),
        P(),
        P(),
        P(),
    )
    out_specs = P("mem", None, "lat", None, None)
    return jax.shard_map(
        on_device, mesh=mesh, in_specs=in_specs, out_specs=out_specs, check_vma=False
    )
```

```python
import functools

import jax
import jax.numpy as jnp
from jax import lax
from jax.experimental import pallas as pl
from jax.experimental.pallas import tpu as pltpu
from jax.sharding import PartitionSpec as P

ROWS = 4
LEV = 4
FIELDS = 5
GROUP = 4
PAD = 1
PARTS = 4
VMEM_LIMIT = 48 * 1024 * 1024
VMEM = pl.BlockSpec(memory_space=pltpu.VMEM)
SMEM = pl.BlockSpec(memory_space=pltpu.SMEM)


def pick_kernel(ids_ref, states_ref, cell_ref, frac_ref, out_ref, table_ref):
    odd = lax.axis_index("lat") % 2
    make_table(odd, cell_ref, frac_ref, table_ref.at[0])
    make_table(1 - odd, cell_ref, frac_ref, table_ref.at[1])
    for i in range(out_ref.shape[0]):
        out_ref[i] = states_ref[ids_ref[0, i]]


def pick(states, src_ids, cell, frac, points):
    return pl.pallas_call(
        pick_kernel,
        out_shape=(
            jax.ShapeDtypeStruct((src_ids.shape[1],) + states.shape[1:], states.dtype),
            jax.ShapeDtypeStruct((2, 6 * points, 2 * cell.shape[1]), jnp.float32),
        ),
        in_specs=[SMEM, VMEM, VMEM, VMEM],
        out_specs=(VMEM, VMEM),
        name="pick",
    )(src_ids, states, cell, frac)


def halves(a):
    big = a.astype(jnp.bfloat16).astype(jnp.float32)
    return big, (a - big).astype(jnp.bfloat16).astype(jnp.float32)


def make_table(pair, cell_ref, frac_ref, table_ref):
    points, nlon = table_ref.shape[0] // 6, cell_ref.shape[1]
    point = lax.broadcasted_iota(jnp.int32, (points, nlon), 0)
    cell = jnp.broadcast_to(cell_ref[...], (points, nlon))
    frac = jnp.broadcast_to(frac_ref[...], (points, nlon))
    table = jnp.where(cell == point, 1.0 - frac, 0.0) + jnp.where(cell + 1 == point, frac, 0.0)
    low, high = [], []
    for i in range(2):
        t = ((2 * pair + i).astype(jnp.float32) + 0.5) / ROWS
        low.append((1.0 - t) * table)
        high.append(t * table)
    both = jnp.concatenate([jnp.concatenate(low, axis=1), jnp.concatenate(high, axis=1)], axis=0)
    big, small = halves(both)
    table_ref[:2 * points] = big
    table_ref[2 * points:4 * points] = small
    table_ref[4 * points:] = big


def make_weights(coarse_ref, table_ref, weights_ref):
    members = weights_ref.shape[0]
    table = table_ref[...]
    for k in range(members):
        big, small = halves(coarse_ref[pl.ds(k, table.shape[0] // 3, stride=members), :])
        rows = jnp.concatenate([big, big, small], axis=0)
        product = lax.dot_general(rows, table, (((0,), (0,)), ((), ())), preferred_element_type=jnp.float32)
        weights_ref[k] = product.reshape(weights_ref.shape[1:])


def analysis_kernel(facing, block, *refs):
    coarse_ref, table_ref, sources_ref, out_ref, send_ref, weights_ref, wide_ref = refs
    odd = lax.axis_index("lat") % 2
    pair = odd if facing else 1 - odd
    count = sources_ref.shape[0]
    sources = count // FIELDS
    members = weights_ref.shape[0]
    half, nlon = out_ref.shape[1:]
    make_weights(coarse_ref, table_ref.at[0 if facing else 1], weights_ref)
    upper = lax.broadcasted_iota(jnp.int32, (half, nlon), 0) < LEV
    later = jnp.full((half, nlon), pair, jnp.int32) != 0
    for i in range(count):
        whole = sources_ref[i].astype(jnp.float32)
        wide_ref[i] = jnp.where(later, whole[half:], whole[:half])
    near = upper != later

    def some_members(b, carry):
        totals = [[None] * FIELDS for _ in range(block)]
        for s in range(sources):
            fields = [wide_ref[s * FIELDS + f] for f in range(FIELDS)]
            for j in range(block):
                row = weights_ref.at[b * block + j, s // 8]
                low, high = [
                    jnp.broadcast_to(row[s % 8:s % 8 + 1, i * nlon:(i + 1) * nlon], (half, nlon)) for i in range(2)
                ]
                w = jnp.where(upper, low, high)
                for f in range(FIELDS):
                    term = w * fields[f]
                    totals[j][f] = term if s == 0 else totals[j][f] + term
        items = [totals[j][f] for j in range(block) for f in range(FIELDS)]
        for i, item in enumerate(items):
            out_ref[b * len(items) + i] = item
        for i in range(0, len(items), 4):
            tile = (b * len(items) + i) // 4 * 3
            four = items[i:i + 4]
            rest = [a - a.astype(jnp.bfloat16).astype(jnp.float32) for a in four]
            rest = [jnp.where(near, rest[j], swap(rest[j + 1])) for j in (0, 2)]
            for j, two in enumerate((four[:2], four[2:], rest)):
                send_ref[tile + j] = jnp.concatenate(two, axis=0).astype(jnp.bfloat16)
        return carry

    if facing:
        send_ref[send_ref.shape[0] - PAD:] = jnp.zeros((PAD, 2 * half, nlon), jnp.bfloat16)
    lax.fori_loop(0, members // block, some_members, 0)


def receive(near, send_ref, out_ref):
    half = out_ref.shape[1]

    def four(g, carry):
        tiles = [send_ref[3 * g + j].astype(jnp.float32) for j in range(3)]
        for i in range(4):
            rest = tiles[2][i // 2 * half:(i // 2 + 1) * half]
            rest = jnp.where(near, swap(rest) if i % 2 else rest, 0.0)
            out_ref[4 * g + i] = tiles[i // 2][i % 2 * half:(i % 2 + 1) * half] + rest
        return carry

    lax.fori_loop(0, out_ref.shape[0] // 4, four, 0, unroll=5)


def analyse(facing, coarse, table, sources, members):
    nlon = sources.shape[2]
    half = ROWS * LEV // 2
    count = sources.shape[0]
    return pl.pallas_call(
        functools.partial(analysis_kernel, facing, 4),
        out_shape=(
            jax.ShapeDtypeStruct((members * FIELDS, half, nlon), jnp.float32),
            jax.ShapeDtypeStruct((members * FIELDS // 4 * 3 + (PAD if facing else 0), 2 * half, nlon), jnp.bfloat16),
        ),
        in_specs=[VMEM] * 3,
        out_specs=(VMEM, VMEM),
        scratch_shapes=[
            pltpu.VMEM((members, count // FIELDS // 8, 8, 2 * nlon), jnp.float32),
            pltpu.VMEM((count, half, nlon), jnp.float32),
        ],
        compiler_params=pltpu.CompilerParams(vmem_limit_bytes=VMEM_LIMIT),
        cost_estimate=pl.CostEstimate(flops=2 * 10**10, bytes_accessed=2 * 10**7, transcendentals=0),
        name="analysis_outer" if facing else "analysis_inner",
    )(coarse, table, sources)


def constants(viscosity_ref, half, nlon):
    upper = lax.broadcasted_iota(jnp.int32, (half, nlon), 0) < LEV
    spread = 0.25 * jnp.concatenate([viscosity_ref[...]] * 2, axis=0)
    odd = jnp.full((half, nlon), lax.axis_index("lat") % 2, jnp.int32) != 0
    return upper, spread, odd


def swap(a):
    return pltpu.roll(a, LEV, 0)


def choose(mask, a, b):
    return [jnp.where(mask, x, y) for x, y in zip(a, b)]


def advance(spread, centre, north, south):
    stay = 1.0 - 4.0 * spread
    west = [pltpu.roll(a, 1, 1) for a in centre]
    east = [pltpu.roll(a, a.shape[1] - 1, 1) for a in centre]
    dx = [e - w for e, w in zip(east, west)]
    dy = [n - s for n, s in zip(north, south)]
    u, v = centre[0] * -0.125, centre[1] * -0.125
    out = []
    for f in range(FIELDS):
        around = (east[f] + west[f]) + (north[f] + south[f])
        out.append(stay * centre[f] + spread * around + (u * dx[f] + v * dy[f]))
    out[0] = out[0] - 0.125 * dx[2]
    out[1] = out[1] - 0.125 * dy[2]
    out[2] = out[2] - 0.125 * (dx[0] + dy[1])
    return out


def begin_kernel(group, viscosity_ref, sent_ref, inner_ref, outer_ref, first_ref, last_ref, near_ref, inside_ref):
    count, half, nlon = inner_ref.shape
    upper, spread, odd = constants(viscosity_ref, half, nlon)
    receive(upper != odd, sent_ref, inside_ref)
    fields = range(FIELDS)

    def one_member(k):
        base = k * FIELDS
        outer = [outer_ref[base + f] for f in fields]
        inner = [inner_ref[base + f] for f in fields]
        inside = [swap(inside_ref[base + f]) for f in fields]
        first, last = choose(odd, inner, outer), choose(odd, outer, inner)
        before = [jnp.where(odd, a, 0.0) for a in inside]
        after = [jnp.where(odd, 0.0, a) for a in inside]
        sf, sl = [swap(a) for a in first], [swap(a) for a in last]
        middle = choose(upper, sf, sl)
        first1 = advance(spread, first, middle, choose(upper, before, sf))
        last1 = advance(spread, last, choose(upper, sl, after), middle)
        near = choose(upper, sl, sf)
        for f in fields:
            first_ref[base + f] = first1[f]
            last_ref[base + f] = last1[f]
            near_ref[base + f] = near[f]

    def some(i, carry):
        for j in range(group):
            one_member(i * group + j)
        return carry

    lax.fori_loop(0, count // FIELDS // group, some, 0)


def begin(viscosity, inside, inner, outer):
    return pl.pallas_call(
        functools.partial(begin_kernel, GROUP),
        out_shape=[jax.ShapeDtypeStruct(inner.shape, jnp.float32)] * 4,
        in_specs=[VMEM] * 4,
        out_specs=[VMEM] * 4,
        compiler_params=pltpu.CompilerParams(vmem_limit_bytes=VMEM_LIMIT),
        cost_estimate=pl.CostEstimate(flops=1, bytes_accessed=1, transcendentals=0),
        name="begin",
    )(viscosity, inside, inner, outer)


def finish_kernel(
    group, viscosity_ref, sent_ref, inside_ref, outer_ref, first_ref, last_ref, near_ref,
    out_ref, outside_ref, result_ref, sem
):
    count, half, nlon = near_ref.shape
    members = count // FIELDS
    upper, spread, odd = constants(viscosity_ref, half, nlon)
    lat = lax.axis_index("lat")
    keep = jnp.where(upper, lax.axis_size("lat") - 1 - lat, lat) != 0
    here = upper != odd
    receive(upper == odd, sent_ref, outside_ref)
    sign = jnp.where(odd, 0.125, -0.125)
    fields = range(FIELDS)

    def one_member(k):
        base = k * FIELDS
        outside = [outside_ref[base + f] for f in fields]
        inside = [inside_ref[base + f] for f in fields]
        first1 = [first_ref[base + f] for f in fields]
        last1 = [last_ref[base + f] for f in fields]
        near = [near_ref[base + f] for f in fields]
        edge = choose(here, inside, outside)
        beyond = [swap(a) for a in choose(here, outside, inside)]
        added = [jnp.where(here, swap(a), 0.0) for a in edge]
        weight = spread - sign * outer_ref[base + 1]
        more = [weight * a for a in added]
        more[1] = more[1] - sign * added[2]
        more[2] = more[2] - sign * added[1]
        first1 = [jnp.where(odd, a, a + m) for a, m in zip(first1, more)]
        last1 = [jnp.where(odd, a + m, a) for a, m in zip(last1, more)]
        edge1 = advance(spread, edge, choose(upper, beyond, near), choose(upper, near, beyond))
        edge1 = [jnp.where(keep, a, 0.0) for a in edge1]
        sf, sl, se = [swap(a) for a in first1], [swap(a) for a in last1], [swap(a) for a in edge1]
        middle = choose(upper, sf, sl)
        first2 = advance(spread, first1, middle, choose(upper, se, sf))
        last2 = advance(spread, last1, choose(upper, sl, se), middle)
        for f in fields:
            result_ref[base + f, :half, :] = first2[f]
            result_ref[base + f, half:, :] = last2[f]

    parts = sem.shape[0]
    copies = []
    for part in range(parts):
        def some(i, carry, part=part):
            for j in range(group):
                one_member(part * (members // parts) + i * group + j)
            return carry

        lax.fori_loop(0, members // parts // group, some, 0)
        rows = pl.ds(part * (count // parts), count // parts)
        copy = pltpu.make_async_copy(result_ref.at[rows], out_ref.at[rows], sem.at[part])
        copy.start()
        copies.append(copy)
    for copy in copies:
        copy.wait()


def finish(viscosity, outside, inside, outer, first, last, near):
    count, half, nlon = near.shape
    return pl.pallas_call(
        functools.partial(finish_kernel, GROUP),
        out_shape=jax.ShapeDtypeStruct((count, 2 * half, nlon), jnp.float32),
        in_specs=[VMEM] * 7,
        out_specs=pl.BlockSpec(memory_space=pl.ANY),
        scratch_shapes=[
            pltpu.VMEM((count, half, nlon), jnp.float32),
            pltpu.VMEM((count, 2 * half, nlon), jnp.float32),
            pltpu.SemaphoreType.DMA((PARTS,)),
        ],
        compiler_params=pltpu.CompilerParams(vmem_limit_bytes=VMEM_LIMIT),
        name="finish",
    )(viscosity, outside, inside, outer, first, last, near)


def on_device(states, src_ids, coarse_w, lon_cell, lon_frac, viscosity):
    members, fields, rows, lev, nlon = states.shape
    size = lax.axis_size("lat")
    coarse = jnp.swapaxes(coarse_w, 2, 3)
    coarse = coarse.reshape(-1, coarse.shape[3])
    picked, table = pick(
        states.reshape(members, fields, rows * lev, nlon), src_ids, lon_cell[None], lon_frac[None], coarse_w.shape[1])
    sources = lax.all_gather(picked, "mem")
    sources = sources.reshape(-1, rows * lev, nlon)
    across = [(i, i + 1) for i in range(1, size - 1, 2)]
    across += [(j, i) for i, j in across]
    within = [(i, i + 1) for i in range(0, size, 2)]
    within += [(j, i) for i, j in within]
    outer, send = analyse(True, coarse, table, sources, members)
    outside = lax.ppermute(send, "lat", across)
    inner, send = analyse(False, coarse, table, sources, members)
    inside = lax.ppermute(send, "lat", within)
    first, last, near, inside = begin(viscosity, inside, inner, outer)
    out = finish(viscosity, outside, inside, outer, first, last, near)
    return out.reshape(members, fields, rows, lev, nlon)


def solution(mesh):
    in_specs = (
        P("mem", None, "lat", None, None),
        P("mem", None),
        P("lat", None, None, "mem"),
        P(),
        P(),
        P(),
    )
    out_specs = P("mem", None, "lat", None, None)
    return jax.shard_map(
        on_device, mesh=mesh, in_specs=in_specs, out_specs=out_specs, check_vma=False
    )
```
